256 devices in a mesh: section: 8 (over z_lo, core), seg: 32 (over y, z_hi, x).
Axes of the slice: x: 4, y: 4, z: 8 (z_hi: 2, z_lo: 4; z = z_hi * 4 + z_lo), core: 2. Of those that a mesh axis runs over, the one named last changes fastest.
Arguments:
- partition_entry_vectors: bfloat16 [8, 4096, 2048], P('section', 'seg'), may hold values from -6 to 6
- stored_recall_contents: bfloat16 [8, 32, 32, 2048], P('section', 'seg'), may hold values from -6 to 6
- probe_mapping_matrix: bfloat16 [8, 2048, 2048], P('section'), may hold values from -0.125 to 0.125
- entry_rescaling_gain: bfloat16 [8, 2048], P('section'), may hold values from 0.5 to 1.5
- recall_cell_probes: bfloat16 [8, 32, 2048], P('section'), may hold values from -6 to 6
- channel_sharpness: float32 [8, 16], P('section'), may hold values from 4 to 20
- cell_channel_persistence: float32 [8, 32, 32, 16], P('section', 'seg'), may hold values from 0.001 to 1
- piece_genuine_tokens: int32 [32], P('seg'), may hold values from 16 to 128, as said below
- closing_result_slope: bfloat16 [4096, 2048], P('seg'), may hold values from -6 to 6
Outputs:
- hidden_grads: bfloat16 [8, 4096, 2048], P('section', 'seg')
- memory_grads: float32 [8, 32, 32, 2048], P('section', 'seg')
The draws below stay inside these ranges and needn't reach their ends.
Inputs may be any that keep to these rules, and one draw needn't show every extreme that they name: `piece_genuine_tokens`: the first segment is full.
All inputs are finite; a program needn't handle non-finite values.
Results may differ from the reference program's by a relative error of at most 0.024.
Values may be sent and summed in bfloat16 or wider, within the bound.
No kernel may reach another device: no remote copies, remote signals or barrier semaphores. Data moves between devices by JAX's collectives and lax.ppermute only.
A program may use at most 128 MiB of HBM per device.

```python
import math
import jax
import jax.numpy as jnp
from jax import lax

D = 2048
HEAD_SIZE = 128
MEM = 32
SEG_ROWS = 128
FOCUS_CHANNELS = 16
DEPTH_PARTITIONS = 8
TEXT_PIECES = 32
TOKENS = 4096


def draw_cell_channel_persistence(key, part):
    key = jax.random.fold_in(key, 7)
    stochastic_seed_sequence = jax.random.split(key, 6)
    slow_share = 0.5
    slow_heads = jax.random.uniform(stochastic_seed_sequence[0], (DEPTH_PARTITIONS, 1, 1, FOCUS_CHANNELS)) < slow_share
    slow_rate = jnp.exp(jax.random.uniform(stochastic_seed_sequence[1], (DEPTH_PARTITIONS, 1, MEM, FOCUS_CHANNELS), minval=math.log(0.05), maxval=math.log(1.1))) / TEXT_PIECES
    fast_rate = jnp.exp(jax.random.uniform(stochastic_seed_sequence[2], (DEPTH_PARTITIONS, 1, MEM, FOCUS_CHANNELS), minval=math.log(0.7), maxval=math.log(3.0)))
    erasure_speed = jnp.where(slow_heads, slow_rate, fast_rate)
    scaling_factor = jnp.exp(jax.random.uniform(stochastic_seed_sequence[3], (DEPTH_PARTITIONS, TEXT_PIECES, MEM, FOCUS_CHANNELS), minval=math.log(0.5), maxval=math.log(2.0)))
    spike_tally = jax.random.uniform(stochastic_seed_sequence[4], (DEPTH_PARTITIONS, TEXT_PIECES, 1, 1)) < 3.0 / TEXT_PIECES
    preserved_share = jax.random.uniform(stochastic_seed_sequence[5], (DEPTH_PARTITIONS, TEXT_PIECES, 1, 1), minval=0.5, maxval=0.8)
    return (jnp.exp(-erasure_speed * scaling_factor) * jnp.where(spike_tally, preserved_share, 1.0)).astype(jnp.float32)


def draw_piece_genuine_tokens(key, part):
    key = jax.random.fold_in(key, 9)
    stochastic_seed_sequence = jax.random.split(key, 2)
    ending = jax.random.randint(stochastic_seed_sequence[0], (TEXT_PIECES,), 0, 4) == 0
    short_length = jax.random.randint(stochastic_seed_sequence[1], (TEXT_PIECES,), SEG_ROWS // 8, SEG_ROWS + 1)
    lengths = jnp.where(ending, short_length, SEG_ROWS)
    return lengths.at[0].set(SEG_ROWS).astype(jnp.int32)


def steps_of(rng, extent, cuts, low, high):
    def one(dim, blocks):
        steps = jax.random.uniform(jax.random.fold_in(jax.random.fold_in(rng, 6), dim), (blocks,), jnp.float32, low / len(cuts), high / len(cuts))
        return jnp.repeat(jnp.exp(steps), extent[dim] // blocks).reshape((-1,) + (1,) * (len(extent) - dim - 1))

    level = one(*cuts[0])
    for cut in cuts[1:]:
        level = level * one(*cut)
    return level


def noise(own_key, extent, spread, reach, cuts=(), held_as=jnp.bfloat16):
    result = spread * jax.random.normal(own_key, extent, jnp.float32)
    if cuts:
        result = result * steps_of(own_key, extent, cuts, -0.22, 0.18)
    return jnp.clip(result, -reach, reach).astype(held_as)


def setup_inputs(seed: int = 0) -> dict:
    streams_of = jax.random.split(jax.random.key(seed), 10)
    return {
        "partition_entry_vectors": noise(streams_of[0], (DEPTH_PARTITIONS, TOKENS, D), 1.0, 6.0, ((0, 8), (1, 32))),
        "stored_recall_contents": noise(streams_of[1], (DEPTH_PARTITIONS, TEXT_PIECES, MEM, D), 1.0, 6.0, ((0, 8), (1, 32))),
        "probe_mapping_matrix": noise(streams_of[2], (DEPTH_PARTITIONS, D, D), D ** -0.5, 0.125, ((0, 8),)),
        "entry_rescaling_gain": jnp.clip(1.0 + 0.1 * jax.random.normal(streams_of[3], (DEPTH_PARTITIONS, D), jnp.float32), 0.5, 1.5).astype(jnp.bfloat16),
        "recall_cell_probes": noise(streams_of[4], (DEPTH_PARTITIONS, MEM, D), 1.0, 6.0, ((0, 8),)),
        "channel_sharpness": jnp.clip(jnp.exp(math.log(20.0) - 1.609438 * jax.random.uniform(streams_of[5], (DEPTH_PARTITIONS, FOCUS_CHANNELS), jnp.float32) ** steps_of(streams_of[5], (DEPTH_PARTITIONS, FOCUS_CHANNELS), ((0, 8),), -0.2, 0.2)), 4.0, 20.0),
        "cell_channel_persistence": draw_cell_channel_persistence(jax.random.fold_in(streams_of[9], 71), 0),
        "piece_genuine_tokens": draw_piece_genuine_tokens(jax.random.fold_in(streams_of[9], 71), 0),
        "closing_result_slope": noise(streams_of[8], (TOKENS, D), 1.0, 6.0, ((0, 32),)),
    }


norm_eps = 1e-05
head_eps = 1e-06
highest = lax.Precision.HIGHEST

def split_heads(matrix):
    return matrix.reshape(matrix.shape[0], -1, HEAD_SIZE)

def inverse_norm(matrix):
    head_parts = split_heads(matrix.astype(jnp.float32))
    return lax.rsqrt(lax.optimization_barrier(jnp.mean(head_parts * head_parts, axis=-1)) + head_eps).T

def normalize_project(tokens_in, gain_row, weight):
    values = tokens_in.astype(jnp.float32)
    row_scale = lax.rsqrt(lax.optimization_barrier(jnp.mean(values * values, axis=-1, keepdims=True)) + norm_eps)
    normed = (values * row_scale * gain_row.astype(jnp.float32)).astype(jnp.bfloat16)
    query_rows = jnp.dot(normed, weight, preferred_element_type=jnp.float32).astype(jnp.bfloat16)
    return (normed, query_rows)

def memory_read(query_rows, memory, smoothing_level):
    query_heads = split_heads(query_rows.astype(jnp.float32))
    memory_heads = split_heads(memory)
    raw_scores = jnp.einsum('rhe,mhe->hrm', query_heads, memory_heads, precision=highest)
    scores = raw_scores * (smoothing_level / HEAD_SIZE)[:, None, None] * inverse_norm(query_rows)[:, :, None] * inverse_norm(memory)[:, None, :]
    weights = jnp.exp(scores)
    weights = (weights / lax.optimization_barrier(jnp.sum(weights, axis=-1, keepdims=True))).astype(jnp.bfloat16)
    mixed_rows = jnp.einsum('hrm,mhe->rhe', weights.astype(jnp.float32), memory_heads, precision=highest)
    return mixed_rows.reshape(query_rows.shape[0], -1)

def memory_write(query_rows, normed, queries_mem, smoothing_level, valid_rows):
    query_heads = split_heads(query_rows.astype(jnp.float32))
    slot_heads = split_heads(queries_mem.astype(jnp.float32))
    value_heads = split_heads(normed.astype(jnp.float32))
    raw_scores = jnp.einsum('mhe,rhe->hmr', slot_heads, query_heads, precision=highest)
    scores = raw_scores * (smoothing_level / HEAD_SIZE)[:, None, None] * inverse_norm(queries_mem)[:, :, None] * inverse_norm(query_rows)[:, None, :]
    weights = jnp.exp(scores) * valid_rows[None, None, :]
    weights = (weights / lax.optimization_barrier(jnp.sum(weights, axis=-1, keepdims=True))).astype(jnp.bfloat16)
    written = jnp.einsum('hmr,rhe->mhe', weights.astype(jnp.float32), value_heads, precision=highest)
    return written.reshape(queries_mem.shape[0], -1)

def reference(partition_entry_vectors, stored_recall_contents, probe_mapping_matrix, entry_rescaling_gain, recall_cell_probes, channel_sharpness, cell_channel_persistence, piece_genuine_tokens, closing_result_slope):
    valid_mask = (jnp.arange(SEG_ROWS)[None, :] < piece_genuine_tokens[:, None]).astype(jnp.float32)
    inputs = partition_entry_vectors.reshape(DEPTH_PARTITIONS, TEXT_PIECES, SEG_ROWS, D)
    out_grad = (closing_result_slope.astype(jnp.float32).reshape(TEXT_PIECES, SEG_ROWS, D) * valid_mask[:, :, None]).astype(jnp.bfloat16)
    hidden_list = [None] * DEPTH_PARTITIONS
    memory_list = [None] * DEPTH_PARTITIONS
    for partition_ordinal in range(DEPTH_PARTITIONS - 1, -1, -1):
        weight = probe_mapping_matrix[partition_ordinal]
        gain_row = entry_rescaling_gain[partition_ordinal]
        queries_mem = recall_cell_probes[partition_ordinal]
        smoothing_level = channel_sharpness[partition_ordinal]
        widened = jnp.repeat(cell_channel_persistence[partition_ordinal], HEAD_SIZE, axis=2)

        def read_part(record):
            tokens_in, memory, cotangent = record
            normed, query_rows = normalize_project(tokens_in, gain_row, weight)
            _, pullback = jax.vjp(lambda query_in, memory_in: memory_read(query_in, memory_in, smoothing_level), query_rows, memory)
            return pullback(cotangent.astype(jnp.float32))
        query_grad, read_memgrad = lax.map(read_part, (inputs[partition_ordinal], stored_recall_contents[partition_ordinal].astype(jnp.float32), out_grad))
        following = (jnp.concatenate([read_memgrad[1:], jnp.zeros_like(read_memgrad[:1])]), jnp.concatenate([widened[1:], jnp.zeros_like(widened[:1])]))

        def carry_back(running, record):
            read_term, erasure_speed = record
            updated = read_term + erasure_speed * running
            return (updated, updated)
        _, memory_grad = lax.scan(carry_back, jnp.zeros((MEM, D), jnp.float32), following, reverse=True)

        def finish_part(record):
            tokens_in, cotangent, grad_read, grad_memory, erasure_speed, valid_rows = record
            (normed, query_rows), pull_front = jax.vjp(lambda tokens_held: normalize_project(tokens_held, gain_row, weight), tokens_in)
            _, pull_write = jax.vjp(lambda query_in, normed_in: memory_write(query_in, normed_in, queries_mem, smoothing_level, valid_rows), query_rows, normed)
            grad_query, grad_normed = pull_write((1.0 - erasure_speed) * grad_memory)
            grad_tokens, = pull_front((grad_normed, grad_read + grad_query))
            return (grad_tokens.astype(jnp.float32) + cotangent.astype(jnp.float32)).astype(jnp.bfloat16)
        hidden = lax.map(finish_part, (inputs[partition_ordinal], out_grad, query_grad, memory_grad, widened, valid_mask))
        hidden_list[partition_ordinal] = hidden.reshape(TOKENS, D)
        memory_list[partition_ordinal] = memory_grad
        out_grad = hidden
    return (jnp.stack(hidden_list), jnp.stack(memory_list))
```

```python
import jax
import jax.numpy as jnp
from jax import lax
from jax.experimental import pallas as pl
from jax.experimental.pallas import tpu as pltpu
from jax.sharding import PartitionSpec as P

D = 2048
HEAD = 128
HEADS = 16
MEM = 32
ROWS = 128
GROUPS = 4
GF = 512
GC = 128
SEGS = 32
ROW = 4
BLOCKS = SEGS // ROW
SECTIONS = 8
AXES = ("section", "seg")

f32 = jnp.float32
bf16 = jnp.bfloat16
norm_eps = 1e-05
head_eps = 1e-06

VMEM = pl.BlockSpec(memory_space=pltpu.VMEM)
SMEM = pl.BlockSpec(memory_space=pltpu.SMEM)
HBM = pl.BlockSpec(memory_space=pl.ANY)


def dot_nn(a, b):
    return lax.dot_general(a, b, (((1,), (0,)), ((), ())), preferred_element_type=f32)


def dot_nt(a, b):
    return lax.dot_general(a, b, (((1,), (1,)), ((), ())), preferred_element_type=f32)


def dot_tn(a, b):
    return lax.dot_general(a, b, (((0,), (0,)), ((), ())), preferred_element_type=f32)


def two_part(value):
    high = value.astype(bf16)
    return high, (value - high.astype(f32)).astype(bf16)


def slot_ones():
    left = lax.broadcasted_iota(jnp.int32, (GC, GC), 0) // MEM
    right = lax.broadcasted_iota(jnp.int32, (GC, GC), 1) // MEM
    return (left == right).astype(f32).astype(bf16)


def sum_slots(value, ones):
    high, low = two_part(value)
    return dot_nn(high, ones) + dot_nn(low, ones)


def spread(parts, rows):
    lane = lax.broadcasted_iota(jnp.int32, (rows, GC), 1) // MEM
    out = jnp.broadcast_to(parts[3], (rows, GC))
    for i in (2, 1, 0):
        out = jnp.where(lane == i, parts[i], out)
    return out


def sharp_row(sharp_ref, g):
    return spread([sharp_ref[0, 4 * g + i] * (1.0 / HEAD) for i in range(4)], 1)


def prepare_kernel(
    x_ref, w_ref, gain_ref, m_ref, p_ref, sharp_ref, count_ref,
    n_ref, qh_ref, invq_ref, rs_ref, bdm_ref, bdmh_ref, bdph_ref, invm_ref, wr_ref, ww_ref,
    bdp_ref,
):
    x = x_ref[...].astype(f32)
    rs = lax.rsqrt(jnp.mean(x * x, axis=-1, keepdims=True) + norm_eps)
    rs_ref[...] = jnp.broadcast_to(rs, (ROWS, HEAD))
    n_ref[...] = (x * rs * gain_ref[...].astype(f32)).astype(bf16)
    for ref in (bdm_ref, bdmh_ref, bdph_ref, bdp_ref):
        ref[...] = jnp.zeros_like(ref)
    ones = slot_ones()
    ones_row = jnp.ones((8, GF), bf16)
    valid = (lax.broadcasted_iota(jnp.int32, (ROWS, GC), 0) < count_ref[0]).astype(f32)
    lane = lax.broadcasted_iota(jnp.int32, (ROWS, HEAD), 1)
    lane_m = lax.broadcasted_iota(jnp.int32, (MEM, HEAD), 1)

    def group(g, carry):
        invq_all, invm_all = carry
        cols = pl.ds(pl.multiple_of(g * GF, GF), GF)
        rows = pl.ds(pl.multiple_of(g * GC, GC), GC)
        qb = dot_nn(n_ref[...], w_ref[:, cols]).astype(bf16)
        invs = []
        for i in range(4):
            at = pl.ds(pl.multiple_of(g * GF + i * HEAD, HEAD), HEAD)
            own = pl.ds(pl.multiple_of(g * GC + i * MEM, MEM), MEM)
            here = pl.ds(i * HEAD, HEAD)
            q = qb[:, i * HEAD : (i + 1) * HEAD].astype(f32)
            inv = lax.rsqrt(jnp.mean(q * q, axis=-1, keepdims=True) + head_eps)
            qh_ref[:, at] = (q * inv).astype(bf16)
            invs.append(inv)
            invq_all = jnp.where(lane == 4 * g + i, inv, invq_all)
            m = m_ref[:, at]
            bdm_ref[own, here] = m
            m = m.astype(f32)
            invm = lax.rsqrt(jnp.mean(m * m, axis=-1, keepdims=True) + head_eps)
            invm_all = jnp.where(lane_m == 4 * g + i, invm, invm_all)
            bdmh_ref[own, here] = (m * invm).astype(bf16)
            p = p_ref[:, at]
            bdp_ref[own, here] = p
            p = p.astype(f32)
            invp = lax.rsqrt(jnp.mean(p * p, axis=-1, keepdims=True) + head_eps)
            bdph_ref[own, here] = (p * invp).astype(bf16)
        invq = spread(invs, ROWS)
        sharp = sharp_row(sharp_ref, g)

        def scores(bd):
            square = bd.astype(f32)
            high, low = two_part(square * square)
            mean = (dot_nt(ones_row, high) + dot_nt(ones_row, low))[0:1] * (1.0 / HEAD)
            return dot_nt(qb, bd) * (sharp * lax.rsqrt(mean + head_eps)) * invq

        read = jnp.exp(scores(bdm_ref[rows, :]))
        wr_ref[:, rows] = (read / sum_slots(read, ones)).astype(bf16)
        write = jnp.exp(scores(bdp_ref[rows, :])) * valid
        ww_ref[:, rows] = (write / jnp.sum(write, axis=0, keepdims=True)).astype(bf16)
        return invq_all, invm_all

    invq_all, invm_all = lax.fori_loop(
        0, GROUPS, group, (jnp.zeros((ROWS, HEAD), f32), jnp.zeros((MEM, HEAD), f32))
    )
    invq_ref[...] = invq_all
    invm_ref[...] = invm_all


def pick_lane(ref, h, rows):
    lane = lax.broadcasted_iota(jnp.int32, (rows, HEAD), 1)
    return jnp.sum(jnp.where(lane == h, ref[...], 0.0), axis=-1, keepdims=True)


def read_kernel(g_ref, wr_ref, bdm_ref, bdmh_ref, qh_ref, invm_ref, sharp_ref, rho_ref, ds_ref):
    ones = slot_ones()

    def group(g, carry):
        cols = pl.ds(pl.multiple_of(g * GF, GF), GF)
        rows = pl.ds(pl.multiple_of(g * GC, GC), GC)
        grad = g_ref[:, cols]
        weights = wr_ref[:, rows]
        wide = weights.astype(f32)
        part = wide * dot_nt(grad, bdm_ref[rows, :])
        ds = ((part - wide * sum_slots(part, ones)) * sharp_row(sharp_ref, g)).astype(bf16)
        ds_ref[:, rows] = ds
        direct = dot_tn(weights, grad)
        scored = dot_tn(ds, qh_ref[:, cols])
        for i in range(4):
            at = pl.ds(pl.multiple_of(g * GF + i * HEAD, HEAD), HEAD)
            own = pl.ds(pl.multiple_of(g * GC + i * MEM, MEM), MEM)
            mh = bdmh_ref[own, i * HEAD : (i + 1) * HEAD].astype(f32)
            a = scored[i * MEM : (i + 1) * MEM, i * HEAD : (i + 1) * HEAD]
            b = direct[i * MEM : (i + 1) * MEM, i * HEAD : (i + 1) * HEAD]
            a = a - mh * (jnp.sum(mh * a, axis=-1, keepdims=True) * (1.0 / HEAD))
            rho_ref[:, at] = (b + pick_lane(invm_ref, 4 * g + i, MEM) * a).astype(bf16)
        return carry

    lax.fori_loop(0, GROUPS, group, 0)


def finish_kernel(
    near_ref, reach_ref, carry_ref, keep_ref, g_ref, n_ref, x_ref, gain_ref, ww_ref, ds_ref,
    bdmh_ref, bdph_ref, qh_ref, invq_ref, rs_ref, sharp_ref, w_hbm,
    hidden_ref, mu_ref,
    w_ref, bdd_ref, dq_ref, dn_ref, sem,
):
    fetch = pltpu.make_async_copy(w_hbm, w_ref, sem)
    fetch.start()
    bdd_ref[...] = jnp.zeros_like(bdd_ref)

    def group(g, carry):
        cols = pl.ds(pl.multiple_of(g * GF, GF), GF)
        rows = pl.ds(pl.multiple_of(g * GC, GC), GC)
        mu = near_ref[:, cols] + reach_ref[:, cols] * carry_ref[:, cols].astype(f32)
        mu_ref[:, cols] = mu
        written = (keep_ref[:, cols] * mu).astype(bf16)
        for i in range(4):
            own = pl.ds(pl.multiple_of(g * GC + i * MEM, MEM), MEM)
            bdd_ref[own, i * HEAD : (i + 1) * HEAD] = written[:, i * HEAD : (i + 1) * HEAD]
        bdd = bdd_ref[rows, :]
        weights = ww_ref[:, rows]
        wide = weights.astype(f32)
        part = wide * dot_nt(n_ref[:, cols], bdd)
        ds = (part - wide * jnp.sum(part, axis=0, keepdims=True)) * sharp_row(sharp_ref, g)
        dn_ref[:, cols] = dot_nn(weights, bdd)
        dqh = dot_nn(ds_ref[:, rows], bdmh_ref[rows, :]) + dot_nn(ds.astype(bf16), bdph_ref[rows, :])
        for i in range(4):
            at = pl.ds(pl.multiple_of(g * GF + i * HEAD, HEAD), HEAD)
            qh = qh_ref[:, at].astype(f32)
            a = dqh[:, i * HEAD : (i + 1) * HEAD]
            a = a - qh * (jnp.sum(qh * a, axis=-1, keepdims=True) * (1.0 / HEAD))
            dq_ref[:, at] = (pick_lane(invq_ref, 4 * g + i, ROWS) * a).astype(bf16)
        return carry

    lax.fori_loop(0, GROUPS, group, 0)
    fetch.wait()
    rs = rs_ref[:, 0:1]

    def project(c, total):
        cols = pl.ds(pl.multiple_of(c * GF, GF), GF)
        dn = dn_ref[:, cols] + dot_nt(dq_ref[...], w_ref[cols, :])
        y = dn * gain_ref[:, cols].astype(f32)
        dn_ref[:, cols] = y
        return total + jnp.sum(y * x_ref[:, cols].astype(f32), axis=-1, keepdims=True)

    total = lax.fori_loop(0, GROUPS, project, jnp.zeros((ROWS, 1), f32))
    shift = total * rs * rs * (1.0 / D)

    def close(c, carry):
        cols = pl.ds(pl.multiple_of(c * GF, GF), GF)
        dx = rs * (dn_ref[:, cols] - x_ref[:, cols].astype(f32) * shift)
        hidden_ref[:, cols] = (g_ref[:, cols].astype(f32) + dx).astype(bf16)
        return carry

    lax.fori_loop(0, GROUPS, close, 0)


def call(kernel, outs, ins, scratch=(), flops=0, moved=0):
    return pl.pallas_call(
        kernel,
        out_shape=[jax.ShapeDtypeStruct(shape, kind) for shape, kind in outs],
        in_specs=ins,
        out_specs=[VMEM] * len(outs),
        scratch_shapes=list(scratch),
        compiler_params=pltpu.CompilerParams(vmem_limit_bytes=44 * 1024 * 1024),
        cost_estimate=pl.CostEstimate(flops=flops, bytes_accessed=moved, transcendentals=0),
    )


def place(section, seg):
    return section * SEGS + seg


def row_swap(value, distance):
    return lax.ppermute(
        value, AXES,
        [(place(s, j), place(s, j ^ distance)) for s in range(SECTIONS) for j in range(SEGS)],
    )


def down_row(b):
    return [
        (place(s, b * ROW + i), place(s, (b - 1) * ROW + i))
        for s in range(SECTIONS)
        for i in range(ROW)
    ]


def widen(value):
    return jnp.repeat(value, HEAD, axis=1)


def local(x, memory, weight, gain, probes, sharp, persistence, counts, slope):
    x, memory, weight, probes = x[0], memory[0, 0], weight[0], probes[0]
    decay = persistence[0, 0]
    section = lax.axis_index("section")
    seg = lax.axis_index("seg")
    spot = seg % ROW
    block = seg // ROW

    n, qh, invq, rs, bdm, bdmh, bdph, invm, wr, ww = call(
        prepare_kernel,
        [
            ((ROWS, D), bf16), ((ROWS, D), bf16), ((ROWS, HEAD), f32), ((ROWS, HEAD), f32),
            ((GF, GF), bf16), ((GF, GF), bf16), ((GF, GF), bf16), ((MEM, HEAD), f32),
            ((ROWS, GF), bf16), ((ROWS, GF), bf16),
        ],
        [VMEM] * 5 + [SMEM] * 2,
        [pltpu.VMEM((GF, GF), bf16)],
        flops=2 * ROWS * D * D, moved=10 << 20,
    )(x, weight, gain, memory, probes, sharp, counts)

    other = row_swap(decay, 1)
    pair = decay * other
    far = row_swap(pair, 2)
    one = jnp.ones_like(decay)
    none = jnp.zeros_like(decay)
    odd, high = spot % 2 == 1, spot >= 2
    own1 = widen(jnp.where(odd, other, one))
    got1 = widen(jnp.where(odd, one, decay))
    own2 = widen(jnp.where(high, far, one))
    got2 = widen(jnp.where(high, one, pair))
    near1 = widen(jnp.where(odd, none, one))
    near2 = widen(jnp.where(high, none, jnp.where(odd, one, other)))
    reach = widen(jnp.where(odd, one, other) * jnp.where(high, one, far))
    whole = widen(pair * far)
    keep = widen(1.0 - decay)

    valid = (jnp.arange(ROWS) < counts[0]).astype(f32)
    start = (slope.astype(f32) * valid[:, None]).astype(bf16)

    def read(grad):
        return call(
            read_kernel,
            [((MEM, D), bf16), ((ROWS, GF), bf16)],
            [VMEM] * 6 + [SMEM],
            flops=2 * ROWS * GF * D, moved=4 << 20,
        )(grad, wr, bdm, bdmh, qh, invm, sharp)

    def finish(near, carry, grad, ds):
        return call(
            finish_kernel,
            [((ROWS, D), bf16), ((MEM, D), f32)],
            [VMEM] * 15 + [SMEM, HBM],
            [
                pltpu.VMEM((D, D), bf16), pltpu.VMEM((GF, GF), bf16), pltpu.VMEM((ROWS, D), bf16),
                pltpu.VMEM((ROWS, D), f32), pltpu.SemaphoreType.DMA,
            ],
            flops=2 * ROWS * D * D, moved=12 << 20,
        )(near, reach, carry, keep, grad, n, x, gain, ww, ds, bdmh, bdph, qh, invq, rs, sharp, weight)

    def turn(grad):
        rho, ds = read(grad)
        get1 = row_swap(rho, 1).astype(f32)
        pair_sum = own1 * rho.astype(f32) + got1 * get1
        get2 = row_swap(pair_sum.astype(bf16), 2).astype(f32)
        row_sum = own2 * pair_sum + got2 * get2
        near = near1 * get1 + near2 * get2
        carry = jnp.zeros((MEM, D), bf16)
        for b in range(BLOCKS - 1, 0, -1):
            def step(carry, b=b):
                moving = (row_sum + whole * carry.astype(f32)).astype(bf16)
                return carry + lax.ppermute(moving, AXES, down_row(b))

            carry = lax.cond((block == b) | (block == b - 1), step, lambda c: c, carry)
        return finish(near, carry, grad, ds)

    state = (start, jnp.zeros((MEM, D), f32))
    grad = start
    for active in range(SECTIONS - 1, -1, -1):
        state = lax.cond(section == active, lambda s, g: turn(g), lambda s, g: s, state, grad)
        if active:
            grad = lax.ppermute(
                state[0], AXES, [(place(active, j), place(active - 1, j)) for j in range(SEGS)]
            )
    return state[0][None], state[1][None, None]


def solution(mesh):
    placed = (
        P("section", "seg", None),
        P("section", "seg", None, None),
        P("section", None, None),
        P("section", None),
        P("section", None, None),
        P("section", None),
        P("section", "seg", None, None),
        P("seg"),
        P("seg", None),
    )
    return jax.shard_map(
        local,
        mesh=mesh,
        in_specs=placed,
        out_specs=(P("section", "seg", None), P("section", "seg", None, None)),
        check_vma=False,
    )
```

```python
import functools

import jax
import jax.numpy as jnp
from jax import lax
from jax.experimental import pallas as pl
from jax.experimental.pallas import tpu as pltpu
from jax.sharding import PartitionSpec as P

D = 2048
HEAD = 128
HEADS = 16
MEM = 32
ROWS = 128
GROUPS = 4
GF = 512
GC = 128
SEGS = 32
PAIRS = SEGS // 2
SECTIONS = 8
AXES = ("section", "seg")
OWN, GOT, NEAR, REACH, WHOLE, KEEP, SHARP = (k * HEADS for k in range(7))

f32 = jnp.float32
bf16 = jnp.bfloat16
norm_eps = 1e-05
head_eps = 1e-06

VMEM = pl.BlockSpec(memory_space=pltpu.VMEM)
SMEM = pl.BlockSpec(memory_space=pltpu.SMEM)
HBM = pl.BlockSpec(memory_space=pltpu.HBM)
ANY = pl.BlockSpec(memory_space=pl.ANY)


def dot_nn(a, b):
    return lax.dot_general(a, b, (((1,), (0,)), ((), ())), preferred_element_type=f32)


def dot_nt(a, b):
    return lax.dot_general(a, b, (((1,), (1,)), ((), ())), preferred_element_type=f32)


def dot_tn(a, b):
    return lax.dot_general(a, b, (((0,), (0,)), ((), ())), preferred_element_type=f32)


def two_part(value):
    high = value.astype(bf16)
    return high, (value - high.astype(f32)).astype(bf16)


def slot_ones():
    left = lax.broadcasted_iota(jnp.int32, (GC, GC), 0) // MEM
    right = lax.broadcasted_iota(jnp.int32, (GC, GC), 1) // MEM
    return (left == right).astype(f32).astype(bf16)


def sum_slots(value, ones):
    high, low = two_part(value)
    return dot_nn(high, ones) + dot_nn(low, ones)


def spread(parts, rows):
    lane = lax.broadcasted_iota(jnp.int32, (rows, GC), 1) // MEM
    out = jnp.broadcast_to(parts[3], (rows, GC))
    for i in (2, 1, 0):
        out = jnp.where(lane == i, parts[i], out)
    return out


def sharp_row(coef_ref, g):
    at = SHARP + 4 * g
    return spread([coef_ref[0:1, at + i : at + i + 1] for i in range(4)], 1)


def prepare_kernel(
    x_ref, w_hbm, gain_ref, m_ref, p_ref, slope_ref, sharp_ref, count_ref,
    n_ref, qh_ref, invq_ref, rs_ref, bdm_ref, bdmh_ref, bdph_ref, invm_ref, wr_ref, ww_ref, start_ref,
    bdp_ref, w_ref, sem,
):
    fetch = pltpu.make_async_copy(w_hbm, w_ref, sem)
    fetch.start()
    x = x_ref[...].astype(f32)
    rs = lax.rsqrt(jnp.mean(x * x, axis=-1, keepdims=True) + norm_eps)
    rs_ref[...] = jnp.broadcast_to(rs, (ROWS, HEAD))
    n_ref[...] = (x * rs * gain_ref[...].astype(f32)).astype(bf16)
    for ref in (bdm_ref, bdmh_ref, bdph_ref, bdp_ref):
        ref[...] = jnp.zeros_like(ref)
    ones = slot_ones()
    ones_row = jnp.ones((8, GF), bf16)
    valid = (lax.broadcasted_iota(jnp.int32, (ROWS, GC), 0) < count_ref[0]).astype(f32)
    whole = lax.broadcasted_iota(jnp.int32, (ROWS, D), 0) < count_ref[0]
    start_ref[...] = jnp.where(whole, slope_ref[...].astype(f32), 0.0).astype(bf16)
    fetch.wait()
    lane = lax.broadcasted_iota(jnp.int32, (ROWS, HEAD), 1)
    lane_m = lax.broadcasted_iota(jnp.int32, (MEM, HEAD), 1)

    def group(g, carry):
        invq_all, invm_all = carry
        cols = pl.ds(g * GF, GF)
        rows = pl.ds(g * GC, GC)
        qb = dot_nn(n_ref[...], w_ref[:, cols]).astype(bf16)
        invs = []
        for i in range(4):
            at = pl.ds(g * GF + i * HEAD, HEAD)
            own = pl.ds(g * GC + i * MEM, MEM)
            here = pl.ds(i * HEAD, HEAD)
            q = qb[:, i * HEAD : (i + 1) * HEAD].astype(f32)
            inv = lax.rsqrt(jnp.mean(q * q, axis=-1, keepdims=True) + head_eps)
            qh_ref[:, at] = (q * inv).astype(bf16)
            invs.append(inv)
            invq_all = jnp.where(lane == 4 * g + i, inv, invq_all)
            m = m_ref[:, at]
            bdm_ref[own, here] = m
            m = m.astype(f32)
            invm = lax.rsqrt(jnp.mean(m * m, axis=-1, keepdims=True) + head_eps)
            invm_all = jnp.where(lane_m == 4 * g + i, invm, invm_all)
            bdmh_ref[own, here] = (m * invm).astype(bf16)
            p = p_ref[:, at]
            bdp_ref[own, here] = p
            p = p.astype(f32)
            invp = lax.rsqrt(jnp.mean(p * p, axis=-1, keepdims=True) + head_eps)
            bdph_ref[own, here] = (p * invp).astype(bf16)
        invq = spread(invs, ROWS)
        sharp = spread([sharp_ref[0, 4 * g + i] * (1.0 / HEAD) for i in range(4)], 1)

        def scores(bd):
            square = bd.astype(f32)
            high, low = two_part(square * square)
            mean = (dot_nt(ones_row, high) + dot_nt(ones_row, low))[0:1] * (1.0 / HEAD)
            return dot_nt(qb, bd) * (sharp * lax.rsqrt(mean + head_eps)) * invq

        read = jnp.exp(scores(bdm_ref[rows, :]))
        wr_ref[:, rows] = (read / sum_slots(read, ones)).astype(bf16)
        write = jnp.exp(scores(bdp_ref[rows, :])) * valid
        ww_ref[:, rows] = (write / jnp.sum(write, axis=0, keepdims=True)).astype(bf16)
        return invq_all, invm_all

    invq_all, invm_all = jnp.zeros((ROWS, HEAD), f32), jnp.zeros((MEM, HEAD), f32)
    for g in range(GROUPS):
        invq_all, invm_all = group(g, (invq_all, invm_all))
    invq_ref[...] = invq_all
    invm_ref[...] = invm_all


def blank_kernel(*refs):
    pass


def join_kernel(has_carry, step_ref, sum_any, near_any, coef_any, *refs):
    carry_any = refs[0] if has_carry else None
    moving_hbm, mu_hbm, sum_ref, near_ref, carry_ref, coef_ref, moving_ref, mu_ref, sems = refs[-9:]

    @pl.when(step_ref[0] == 0)
    def _():
        sources = [(coef_any, coef_ref), (sum_any, sum_ref), (near_any, near_ref)]
        if has_carry:
            sources.append((carry_any, carry_ref))
        fetch = [pltpu.make_async_copy(*pair, sems.at[k]) for k, pair in enumerate(sources)]
        leave_moving = pltpu.make_async_copy(moving_ref, moving_hbm, sems.at[4])
        leave_mu = pltpu.make_async_copy(mu_ref, mu_hbm, sems.at[5])
        for copy in fetch:
            copy.start()
        for copy in fetch:
            copy.wait()
        near = coef_ref[:, NEAR : NEAR + 1]
        for h in range(HEADS):
            at = pl.ds(h * HEAD, HEAD)
            moving = sum_ref[:, at]
            mu = near * near_ref[:, at].astype(f32)
            if has_carry:
                carry = carry_ref[:, at].astype(f32)
                reach, whole = (coef_ref[:, c + h : c + h + 1] for c in (REACH, WHOLE))
                moving = (moving.astype(f32) + whole * carry).astype(bf16)
                mu = mu + reach * carry
            moving_ref[:, at] = moving
            mu_ref[:, at] = mu
        leave_moving.start()
        leave_mu.start()
        leave_moving.wait()
        leave_mu.wait()


def combine_kernel(rho_ref, get_ref, coef_ref, out_ref):
    for h in range(HEADS):
        at = pl.ds(h * HEAD, HEAD)
        own = coef_ref[:, OWN + h : OWN + h + 1]
        got = coef_ref[:, GOT + h : GOT + h + 1]
        out_ref[:, at] = (own * rho_ref[:, at].astype(f32) + got * get_ref[:, at].astype(f32)).astype(bf16)


def read_kernel(g_ref, wr_ref, bdm_ref, bdmh_ref, qh_ref, invm_ref, coef_ref, rho_ref, ds_ref):
    ones = slot_ones()

    def group(g, carry):
        cols = pl.ds(g * GF, GF)
        rows = pl.ds(g * GC, GC)
        grad = g_ref[:, cols]
        weights = wr_ref[:, rows]
        wide = weights.astype(f32)
        part = wide * dot_nt(grad, bdm_ref[rows, :])
        ds = ((part - wide * sum_slots(part, ones)) * sharp_row(coef_ref, g)).astype(bf16)
        ds_ref[:, rows] = ds
        direct = dot_tn(weights, grad)
        scored = dot_tn(ds, qh_ref[:, cols])
        for i in range(4):
            at = pl.ds(g * GF + i * HEAD, HEAD)
            own = pl.ds(g * GC + i * MEM, MEM)
            mh = bdmh_ref[own, i * HEAD : (i + 1) * HEAD].astype(f32)
            a = scored[i * MEM : (i + 1) * MEM, i * HEAD : (i + 1) * HEAD]
            b = direct[i * MEM : (i + 1) * MEM, i * HEAD : (i + 1) * HEAD]
            a = a - mh * (jnp.sum(mh * a, axis=-1, keepdims=True) * (1.0 / HEAD))
            rho_ref[:, at] = (b + invm_ref[:, 4 * g + i : 4 * g + i + 1] * a).astype(bf16)
        return carry

    for g in range(GROUPS):
        group(g, 0)


def finish_kernel(
    mu_hbm, coef_ref, g_hbm, n_ref, x_hbm, gain_hbm, ww_ref, ds_ref,
    bdmh_ref, bdph_ref, qh_ref, invq_hbm, rs_hbm, w_hbm,
    hidden_hbm, unused_sum, unused_near,
    w_ref, bdd_ref, dq_ref, dn_ref, g_ref, x_ref, hidden_ref, mu_ref, gain_ref, invq_ref, rs_ref, sems,
):
    fetch_mu = pltpu.make_async_copy(mu_hbm, mu_ref, sems.at[0])
    fetch_w = pltpu.make_async_copy(w_hbm, w_ref, sems.at[1])
    fetch_x = pltpu.make_async_copy(x_hbm, x_ref, sems.at[2])
    fetch_g = pltpu.make_async_copy(g_hbm, g_ref, sems.at[3])
    leave = [
        pltpu.make_async_copy(
            hidden_ref.at[:, pl.ds(c * GF, GF)], hidden_hbm.at[:, pl.ds(c * GF, GF)], sems.at[4 + c]
        )
        for c in range(GROUPS)
    ]
    fetch_gain = pltpu.make_async_copy(gain_hbm, gain_ref, sems.at[4 + GROUPS])
    fetch_invq = pltpu.make_async_copy(invq_hbm, invq_ref, sems.at[5 + GROUPS])
    fetch_rs = pltpu.make_async_copy(rs_hbm, rs_ref, sems.at[6 + GROUPS])
    for copy in (fetch_mu, fetch_invq, fetch_gain, fetch_rs, fetch_x, fetch_g, fetch_w):
        copy.start()
    bdd_ref[...] = jnp.zeros_like(bdd_ref)
    fetch_mu.wait()
    fetch_invq.wait()

    def group(g, carry):
        cols = pl.ds(g * GF, GF)
        rows = pl.ds(g * GC, GC)
        for i in range(4):
            h = 4 * g + i
            at = pl.ds(h * HEAD, HEAD)
            keep = coef_ref[:, KEEP + h : KEEP + h + 1]
            mu = mu_ref[:, at]
            own = pl.ds(g * GC + i * MEM, MEM)
            bdd_ref[own, i * HEAD : (i + 1) * HEAD] = (keep * mu).astype(bf16)
        bdd = bdd_ref[rows, :]
        weights = ww_ref[:, rows]
        wide = weights.astype(f32)
        part = wide * dot_nt(n_ref[:, cols], bdd)
        ds = (part - wide * jnp.sum(part, axis=0, keepdims=True)) * sharp_row(coef_ref, g)
        dn_ref[:, cols] = dot_nn(weights, bdd)
        dqh = dot_nn(ds_ref[:, rows], bdmh_ref[rows, :]) + dot_nn(ds.astype(bf16), bdph_ref[rows, :])
        for i in range(4):
            at = pl.ds(g * GF + i * HEAD, HEAD)
            qh = qh_ref[:, at].astype(f32)
            a = dqh[:, i * HEAD : (i + 1) * HEAD]
            a = a - qh * (jnp.sum(qh * a, axis=-1, keepdims=True) * (1.0 / HEAD))
            dq_ref[:, at] = (invq_ref[:, 4 * g + i : 4 * g + i + 1] * a).astype(bf16)
        return carry

    for g in range(GROUPS):
        group(g, 0)
    fetch_gain.wait()
    fetch_rs.wait()
    fetch_x.wait()
    fetch_g.wait()
    fetch_w.wait()
    rs = rs_ref[:, 0:1]

    def project(c, total):
        cols = pl.ds(c * GF, GF)
        dn = dn_ref[:, cols] + dot_nt(dq_ref[...], w_ref[cols, :])
        y = dn * gain_ref[:, cols].astype(f32)
        dn_ref[:, cols] = y
        return total + jnp.sum(y * x_ref[:, cols].astype(f32), axis=-1, keepdims=True)

    total = jnp.zeros((ROWS, 1), f32)
    for c in range(GROUPS):
        total = project(c, total)
    shift = total * rs * rs * (1.0 / D)

    def close(c, carry):
        cols = pl.ds(c * GF, GF)
        dx = rs * (dn_ref[:, cols] - x_ref[:, cols].astype(f32) * shift)
        hidden_ref[:, cols] = (g_ref[:, cols].astype(f32) + dx).astype(bf16)
        leave[c].start()

    for c in range(GROUPS):
        close(c, 0)
    for copy in leave:
        copy.wait()


def call(kernel, outs, ins, scratch=(), flops=0, moved=0, out=VMEM, aliases={}):
    return pl.pallas_call(
        kernel,
        out_shape=[jax.ShapeDtypeStruct(shape, kind) for shape, kind in outs],
        in_specs=ins,
        out_specs=out if isinstance(out, list) else [out] * len(outs),
        scratch_shapes=list(scratch),
        input_output_aliases=aliases,
        compiler_params=pltpu.CompilerParams(vmem_limit_bytes=44 * 1024 * 1024),
        cost_estimate=pl.CostEstimate(flops=flops, bytes_accessed=moved, transcendentals=0),
    )


def place(section, seg):
    return section * SEGS + seg


def pair_swap(value):
    return lax.ppermute(
        value, AXES, [(place(s, j), place(s, j ^ 1)) for s in range(SECTIONS) for j in range(SEGS)]
    )


def chain_sets(parity):
    return [
        (place(s, 2 * p + i), place(s, 2 * p - 1 - i))
        for s in range(SECTIONS)
        for p in range(1, PAIRS)
        if p % 2 == parity
        for i in range(2)
    ]


def hop_sets(parity):
    return [
        (place(s, j), place(s - 1, j))
        for s in range(1, SECTIONS)
        if s % 2 == parity
        for j in range(SEGS)
    ]


def local(x, memory, weight, gain, probes, sharp, persistence, counts, slope):
    x, memory, weight, probes = x[0], memory[0, 0], weight[0], probes[0]
    decay = persistence[0, 0]
    section = lax.axis_index("section")
    seg = lax.axis_index("seg")
    pair = seg // 2

    n, qh, invq, rs, bdm, bdmh, bdph, invm, wr, ww, start = call(
        prepare_kernel,
        [
            ((ROWS, D), bf16), ((ROWS, D), bf16), ((ROWS, HEAD), f32), ((ROWS, HEAD), f32),
            ((GF, GF), bf16), ((GF, GF), bf16), ((GF, GF), bf16), ((MEM, HEAD), f32),
            ((ROWS, GF), bf16), ((ROWS, GF), bf16), ((ROWS, D), bf16),
        ],
        [VMEM, HBM] + [VMEM] * 4 + [SMEM] * 2,
        [pltpu.VMEM((GF, GF), bf16), pltpu.VMEM((D, D), bf16), pltpu.SemaphoreType.DMA],
        flops=2 * ROWS * D * D, moved=10 << 20,
    )(x, weight, gain, memory, probes, slope, sharp, counts)

    other = pair_swap(decay)
    one = jnp.ones_like(decay)
    none = jnp.zeros_like(decay)
    odd = seg % 2 == 1
    coefs = jnp.concatenate(
        [
            jnp.where(odd, other, one), jnp.where(odd, one, decay), jnp.where(odd, none, one),
            jnp.where(odd, one, other), decay * other, 1.0 - decay,
            jnp.broadcast_to(sharp * (1.0 / HEAD), decay.shape), none,
        ],
        axis=1,
    )

    def read(grad):
        return call(
            read_kernel,
            [((MEM, D), bf16), ((ROWS, GF), bf16)],
            [VMEM] * 7,
            flops=2 * ROWS * GF * D, moved=4 << 20,
        )(grad, wr, bdm, bdmh, qh, invm, coefs)

    def finish(mu, grad, ds):
        return call(
            finish_kernel,
            [((ROWS, D), bf16), ((MEM, D), bf16), ((MEM, D), bf16)],
            [HBM, VMEM, HBM, VMEM, HBM, HBM] + [VMEM] * 5 + [HBM] * 3,
            [
                pltpu.VMEM((D, D), bf16), pltpu.VMEM((GF, GF), bf16), pltpu.VMEM((ROWS, D), bf16),
                pltpu.VMEM((ROWS, D), f32), pltpu.VMEM((ROWS, D), bf16), pltpu.VMEM((ROWS, D), bf16),
                pltpu.VMEM((ROWS, D), bf16), pltpu.VMEM((MEM, D), f32), pltpu.VMEM((1, D), bf16),
                pltpu.VMEM((ROWS, HEAD), f32), pltpu.VMEM((ROWS, HEAD), f32),
                pltpu.SemaphoreType.DMA((7 + GROUPS,)),
            ],
            out=[HBM, ANY, ANY],
            flops=2 * ROWS * D * D, moved=12 << 20,
        )(mu, coefs, grad, n, x, gain, ww, ds, bdmh, bdph, qh, invq, rs, weight)

    def join(step, pair_sum, near, moving, mu, carry=None):
        got = [] if carry is None else [carry]
        count = 4 + len(got)
        return call(
            functools.partial(join_kernel, bool(got)),
            [((MEM, D), bf16), ((MEM, D), f32)],
            [SMEM] + [ANY] * (len(got) + 3) + [HBM] * 2,
            [pltpu.VMEM((MEM, D), bf16)] * 3
            + [
                pltpu.VMEM((MEM, HEAD), f32), pltpu.VMEM((MEM, D), bf16), pltpu.VMEM((MEM, D), f32),
                pltpu.SemaphoreType.DMA((6,)),
            ],
            moved=700 << 10, out=HBM, aliases={count: 0, count + 1: 1},
        )(step, pair_sum, near, coefs, *got, moving, mu)

    def blank(*kinds):
        return call(blank_kernel, kinds, [], out=HBM)()

    def first(grad):
        rho, ds = read(grad)
        near = pair_swap(rho)
        pair_sum = call(combine_kernel, [((MEM, D), bf16)], [VMEM] * 3, moved=400 << 10)(rho, near, coefs)[0]
        return pair_sum, near, ds

    def turn(grad):
        def body(step, held):
            moving, mu, ds, hidden = held
            step_now = jnp.reshape(step, (1,))

            def chain(sets):
                def run():
                    got = (lax.ppermute(moving, AXES, sets),) if sets else ()

                    def finishing():
                        new, *unused = finish(mu, grad, ds)
                        return (*unused, ds, new)

                    pair_sum, near, ds_, hidden_ = lax.cond(
                        step == 0, lambda: first(grad) + (hidden,), finishing
                    )
                    return (*join(step_now, pair_sum, near, moving, mu, *got), ds_, hidden_)
                return run

            sends = step == 1
            chain_to = jnp.where(
                pair == jnp.where(sends, 0, PAIRS - 1), 0, jnp.where((pair % 2 == 1) == sends, 1, 2)
            )
            return tuple(
                lax.switch(chain_to, [chain(None), chain(chain_sets(1)), chain(chain_sets(0))])
            )

        held = blank(((MEM, D), bf16), ((MEM, D), f32), ((ROWS, GF), bf16), ((ROWS, D), bf16))
        held = lax.fori_loop(0, two, body, tuple(held))
        return held[3], held[1]

    def hop(step, held):
        grad, hidden, mu = held
        sends = step == 1
        hop_to = jnp.where(
            section == jnp.where(sends, 0, SECTIONS - 1), 0, jnp.where((section % 2 == 1) == sends, 1, 2)
        )
        grad = lax.switch(
            hop_to,
            [
                lambda: grad,
                lambda: lax.ppermute(hidden, AXES, hop_sets(1)),
                lambda: lax.ppermute(hidden, AXES, hop_sets(0)),
            ],
        )
        hidden, mu = lax.cond(sends, lambda: (hidden, mu), lambda: tuple(turn(grad)))
        return grad, hidden, mu

    two = jnp.minimum(counts[0], 2)
    state = lax.fori_loop(
        0, two, hop, (start, *blank(((ROWS, D), bf16), ((MEM, D), f32)))
    )[1:]
    return state[0][None], state[1][None, None]


def solution(mesh):
    placed = (
        P("section", "seg", None),
        P("section", "seg", None, None),
        P("section", None, None),
        P("section", None),
        P("section", None, None),
        P("section", None),
        P("section", "seg", None, None),
        P("seg"),
        P("seg", None),
    )
    return jax.shard_map(
        local,
        mesh=mesh,
        in_specs=placed,
        out_specs=(P("section", "seg", None), P("section", "seg", None, None)),
        check_vma=False,
    )
```

```python
import functools

import jax
import jax.numpy as jnp
from jax import lax
from jax.experimental import pallas as pl
from jax.experimental.pallas import tpu as pltpu
from jax.sharding import PartitionSpec as P

D = 2048
HEAD = 128
HEADS = 16
MEM = 32
ROWS = 128
GROUPS = 4
GF = 512
GC = 128
SEGS = 32
PAIRS = SEGS // 2
SECTIONS = 8
AXES = ("section", "seg")
OWN, GOT, NEAR, REACH, WHOLE, KEEP, SHARP = (k * HEADS for k in range(7))

f32 = jnp.float32
bf16 = jnp.bfloat16
norm_eps = 1e-05
head_eps = 1e-06

VMEM = pl.BlockSpec(memory_space=pltpu.VMEM)
SMEM = pl.BlockSpec(memory_space=pltpu.SMEM)
HBM = pl.BlockSpec(memory_space=pltpu.HBM)
ANY = pl.BlockSpec(memory_space=pl.ANY)


def dot_nn(a, b):
    return lax.dot_general(a, b, (((1,), (0,)), ((), ())), preferred_element_type=f32)


def dot_nt(a, b):
    return lax.dot_general(a, b, (((1,), (1,)), ((), ())), preferred_element_type=f32)


def dot_tn(a, b):
    return lax.dot_general(a, b, (((0,), (0,)), ((), ())), preferred_element_type=f32)


def two_part(value):
    high = value.astype(bf16)
    return high, (value - high.astype(f32)).astype(bf16)


def slot_ones():
    left = lax.broadcasted_iota(jnp.int32, (GC, GC), 0) // MEM
    right = lax.broadcasted_iota(jnp.int32, (GC, GC), 1) // MEM
    return (left == right).astype(f32).astype(bf16)


def sum_slots(value, ones):
    high, low = two_part(value)
    return dot_nn(high, ones) + dot_nn(low, ones)


def spread(parts, rows):
    lane = lax.broadcasted_iota(jnp.int32, (rows, GC), 1) // MEM
    out = jnp.broadcast_to(parts[3], (rows, GC))
    for i in (2, 1, 0):
        out = jnp.where(lane == i, parts[i], out)
    return out


def sharp_row(coef_ref, g):
    at = SHARP + 4 * g
    return spread([coef_ref[0:1, at + i : at + i + 1] for i in range(4)], 1)


def prepare_kernel(
    x_ref, w_hbm, gain_ref, m_ref, p_ref, slope_ref, sharp_ref, count_ref,
    n_ref, qh_ref, invq_ref, rs_ref, bdm_ref, bdmh_ref, bdph_ref, invm_ref, wr_ref, ww_ref, start_ref,
    bdp_ref, w_ref, sem,
):
    fetch = pltpu.make_async_copy(w_hbm, w_ref, sem)
    fetch.start()
    x = x_ref[...].astype(f32)
    rs = lax.rsqrt(jnp.mean(x * x, axis=-1, keepdims=True) + norm_eps)
    rs_ref[...] = jnp.broadcast_to(rs, (ROWS, HEAD))
    n_ref[...] = (x * rs * gain_ref[...].astype(f32)).astype(bf16)
    for ref in (bdm_ref, bdmh_ref, bdph_ref, bdp_ref):
        ref[...] = jnp.zeros_like(ref)
    ones = slot_ones()
    ones_row = jnp.ones((8, GF), bf16)
    valid = (lax.broadcasted_iota(jnp.int32, (ROWS, GC), 0) < count_ref[0]).astype(f32)
    whole = lax.broadcasted_iota(jnp.int32, (ROWS, D), 0) < count_ref[0]
    start_ref[...] = jnp.where(whole, slope_ref[...].astype(f32), 0.0).astype(bf16)
    fetch.wait()
    lane = lax.broadcasted_iota(jnp.int32, (ROWS, HEAD), 1)
    lane_m = lax.broadcasted_iota(jnp.int32, (MEM, HEAD), 1)

    def group(g, carry):
        invq_all, invm_all = carry
        cols = pl.ds(g * GF, GF)
        rows = pl.ds(g * GC, GC)
        qb = dot_nn(n_ref[...], w_ref[:, cols]).astype(bf16)
        invs = []
        for i in range(4):
            at = pl.ds(g * GF + i * HEAD, HEAD)
            own = pl.ds(g * GC + i * MEM, MEM)
            here = pl.ds(i * HEAD, HEAD)
            q = qb[:, i * HEAD : (i + 1) * HEAD].astype(f32)
            inv = lax.rsqrt(jnp.mean(q * q, axis=-1, keepdims=True) + head_eps)
            qh_ref[:, at] = (q * inv).astype(bf16)
            invs.append(inv)
            invq_all = jnp.where(lane == 4 * g + i, inv, invq_all)
            m = m_ref[:, at]
            bdm_ref[own, here] = m
            m = m.astype(f32)
            invm = lax.rsqrt(jnp.mean(m * m, axis=-1, keepdims=True) + head_eps)
            invm_all = jnp.where(lane_m == 4 * g + i, invm, invm_all)
            bdmh_ref[own, here] = (m * invm).astype(bf16)
            p = p_ref[:, at]
            bdp_ref[own, here] = p
            p = p.astype(f32)
            invp = lax.rsqrt(jnp.mean(p * p, axis=-1, keepdims=True) + head_eps)
            bdph_ref[own, here] = (p * invp).astype(bf16)
        invq = spread(invs, ROWS)
        sharp = spread([sharp_ref[0, 4 * g + i] * (1.0 / HEAD) for i in range(4)], 1)

        def scores(bd):
            square = bd.astype(f32)
            high, low = two_part(square * square)
            mean = (dot_nt(ones_row, high) + dot_nt(ones_row, low))[0:1] * (1.0 / HEAD)
            return dot_nt(qb, bd) * (sharp * lax.rsqrt(mean + head_eps)) * invq

        read = jnp.exp(scores(bdm_ref[rows, :]))
        wr_ref[:, rows] = (read / sum_slots(read, ones)).astype(bf16)
        write = jnp.exp(scores(bdp_ref[rows, :])) * valid
        ww_ref[:, rows] = (write / jnp.sum(write, axis=0, keepdims=True)).astype(bf16)
        return invq_all, invm_all

    invq_all, invm_all = jnp.zeros((ROWS, HEAD), f32), jnp.zeros((MEM, HEAD), f32)
    for g in range(GROUPS):
        invq_all, invm_all = group(g, (invq_all, invm_all))
    invq_ref[...] = invq_all
    invm_ref[...] = invm_all


def blank_kernel(*refs):
    pass


def join_kernel(has_carry, step_ref, sum_any, near_any, coef_any, *refs):
    carry_any = refs[0] if has_carry else None
    moving_hbm, mu_hbm, sum_ref, near_ref, carry_ref, coef_ref, moving_ref, mu_ref, sems = refs[-9:]

    @pl.when(step_ref[0] == 0)
    def _():
        sources = [(coef_any, coef_ref), (sum_any, sum_ref), (near_any, near_ref)]
        if has_carry:
            sources.append((carry_any, carry_ref))
        fetch = [pltpu.make_async_copy(*pair, sems.at[k]) for k, pair in enumerate(sources)]
        halves = [pl.ds(k * (D // 2), D // 2) for k in range(2)]
        leave_moving = [
            pltpu.make_async_copy(moving_ref.at[:, half], moving_hbm.at[:, half], sems.at[4 + k])
            for k, half in enumerate(halves)
        ]
        leave_mu = [
            pltpu.make_async_copy(mu_ref.at[:, half], mu_hbm.at[:, half], sems.at[6 + k])
            for k, half in enumerate(halves)
        ]
        for copy in fetch:
            copy.start()
        for copy in fetch:
            copy.wait()
        near = coef_ref[:, NEAR : NEAR + 1]
        for h in range(HEADS):
            at = pl.ds(h * HEAD, HEAD)
            moving = sum_ref[:, at]
            mu = near * near_ref[:, at].astype(f32)
            if has_carry:
                carry = carry_ref[:, at].astype(f32)
                reach, whole = (coef_ref[:, c + h : c + h + 1] for c in (REACH, WHOLE))
                moving = (moving.astype(f32) + whole * carry).astype(bf16)
                mu = mu + reach * carry
            moving_ref[:, at] = moving
            mu_ref[:, at] = mu
            if (h + 1) % (HEADS // 2) == 0:
                leave_mu[h // (HEADS // 2)].start()
                leave_moving[h // (HEADS // 2)].start()
        for copy in leave_moving + leave_mu:
            copy.wait()


def combine_kernel(rho_ref, get_ref, coef_ref, out_ref):
    for h in range(HEADS):
        at = pl.ds(h * HEAD, HEAD)
        own = coef_ref[:, OWN + h : OWN + h + 1]
        got = coef_ref[:, GOT + h : GOT + h + 1]
        out_ref[:, at] = (own * rho_ref[:, at].astype(f32) + got * get_ref[:, at].astype(f32)).astype(bf16)


def read_kernel(g_ref, wr_ref, bdm_ref, bdmh_ref, qh_ref, invm_ref, coef_ref, rho_ref, ds_ref):
    ones = slot_ones()

    def group(g, carry):
        cols = pl.ds(g * GF, GF)
        rows = pl.ds(g * GC, GC)
        grad = g_ref[:, cols]
        weights = wr_ref[:, rows]
        wide = weights.astype(f32)
        part = wide * dot_nt(grad, bdm_ref[rows, :])
        ds = ((part - wide * dot_nn(part.astype(bf16), ones)) * sharp_row(coef_ref, g)).astype(bf16)
        ds_ref[:, rows] = ds
        direct = dot_tn(weights, grad)
        scored = dot_tn(ds, qh_ref[:, cols])
        for i in range(4):
            at = pl.ds(g * GF + i * HEAD, HEAD)
            own = pl.ds(g * GC + i * MEM, MEM)
            mh = bdmh_ref[own, i * HEAD : (i + 1) * HEAD].astype(f32)
            a = scored[i * MEM : (i + 1) * MEM, i * HEAD : (i + 1) * HEAD]
            b = direct[i * MEM : (i + 1) * MEM, i * HEAD : (i + 1) * HEAD]
            a = a - mh * (jnp.sum(mh * a, axis=-1, keepdims=True) * (1.0 / HEAD))
            rho_ref[:, at] = (b + invm_ref[:, 4 * g + i : 4 * g + i + 1] * a).astype(bf16)
        return carry

    for g in range(GROUPS):
        group(g, 0)


def finish_kernel(
    mu_hbm, coef_ref, g_hbm, n_ref, x_hbm, gain_hbm, ww_ref, ds_ref,
    bdmh_ref, bdph_ref, qh_ref, invq_hbm, rs_hbm, w_hbm,
    hidden_hbm, unused_sum, unused_near,
    w_ref, bdd_ref, dq_ref, dn_ref, g_ref, x_ref, hidden_ref, mu_ref, gain_ref, invq_ref, rs_ref, sems,
):
    fetch_mu = pltpu.make_async_copy(mu_hbm, mu_ref, sems.at[0])
    fetch_w = pltpu.make_async_copy(w_hbm, w_ref, sems.at[1])
    fetch_x = pltpu.make_async_copy(x_hbm, x_ref, sems.at[2])
    fetch_g = pltpu.make_async_copy(g_hbm, g_ref, sems.at[3])
    leave = [
        pltpu.make_async_copy(
            hidden_ref.at[:, pl.ds(c * GF, GF)], hidden_hbm.at[:, pl.ds(c * GF, GF)], sems.at[4 + c]
        )
        for c in range(GROUPS)
    ]
    fetch_gain = pltpu.make_async_copy(gain_hbm, gain_ref, sems.at[4 + GROUPS])
    fetch_invq = pltpu.make_async_copy(invq_hbm, invq_ref, sems.at[5 + GROUPS])
    fetch_rs = pltpu.make_async_copy(rs_hbm, rs_ref, sems.at[6 + GROUPS])
    for copy in (fetch_mu, fetch_invq, fetch_w, fetch_gain, fetch_rs, fetch_x, fetch_g):
        copy.start()
    bdd_ref[...] = jnp.zeros_like(bdd_ref)
    fetch_mu.wait()
    fetch_invq.wait()

    def group(g, carry):
        cols = pl.ds(g * GF, GF)
        rows = pl.ds(g * GC, GC)
        for i in range(4):
            h = 4 * g + i
            at = pl.ds(h * HEAD, HEAD)
            keep = coef_ref[:, KEEP + h : KEEP + h + 1]
            mu = mu_ref[:, at]
            own = pl.ds(g * GC + i * MEM, MEM)
            bdd_ref[own, i * HEAD : (i + 1) * HEAD] = (keep * mu).astype(bf16)
        bdd = bdd_ref[rows, :]
        weights = ww_ref[:, rows]
        wide = weights.astype(f32)
        part = wide * dot_nt(n_ref[:, cols], bdd)
        ds = (part - wide * jnp.sum(part, axis=0, keepdims=True)) * sharp_row(coef_ref, g)
        dn_ref[:, cols] = dot_nn(weights, bdd)
        dqh = dot_nn(ds_ref[:, rows], bdmh_ref[rows, :]) + dot_nn(ds.astype(bf16), bdph_ref[rows, :])
        for i in range(4):
            at = pl.ds(g * GF + i * HEAD, HEAD)
            qh = qh_ref[:, at].astype(f32)
            a = dqh[:, i * HEAD : (i + 1) * HEAD]
            a = a - qh * (jnp.sum(qh * a, axis=-1, keepdims=True) * (1.0 / HEAD))
            dq_ref[:, at] = (invq_ref[:, 4 * g + i : 4 * g + i + 1] * a).astype(bf16)
        return carry

    for g in range(GROUPS):
        group(g, 0)
    fetch_gain.wait()
    fetch_rs.wait()
    fetch_x.wait()
    fetch_g.wait()
    fetch_w.wait()
    rs = rs_ref[:, 0:1]

    def project(c, total):
        cols = pl.ds(c * GF, GF)
        dn = dn_ref[:, cols] + dot_nt(dq_ref[...], w_ref[cols, :])
        y = dn * gain_ref[:, cols].astype(f32)
        dn_ref[:, cols] = y
        return total + jnp.sum(y * x_ref[:, cols].astype(f32), axis=-1, keepdims=True)

    total = jnp.zeros((ROWS, 1), f32)
    for c in range(GROUPS):
        total = project(c, total)
    shift = total * rs * rs * (1.0 / D)

    def close(c, carry):
        cols = pl.ds(c * GF, GF)
        dx = rs * (dn_ref[:, cols] - x_ref[:, cols].astype(f32) * shift)
        hidden_ref[:, cols] = (g_ref[:, cols].astype(f32) + dx).astype(bf16)
        leave[c].start()

    for c in range(GROUPS):
        close(c, 0)
    for copy in leave:
        copy.wait()


def call(kernel, outs, ins, scratch=(), flops=0, moved=0, out=VMEM, aliases={}):
    return pl.pallas_call(
        kernel,
        out_shape=[jax.ShapeDtypeStruct(shape, kind) for shape, kind in outs],
        in_specs=ins,
        out_specs=out if isinstance(out, list) else [out] * len(outs),
        scratch_shapes=list(scratch),
        input_output_aliases=aliases,
        compiler_params=pltpu.CompilerParams(vmem_limit_bytes=44 * 1024 * 1024),
        cost_estimate=pl.CostEstimate(flops=flops, bytes_accessed=moved, transcendentals=0),
    )


def place(section, seg):
    return section * SEGS + seg


def pair_swap(value):
    return lax.ppermute(
        value, AXES, [(place(s, j), place(s, j ^ 1)) for s in range(SECTIONS) for j in range(SEGS)]
    )


def chain_sets(parity):
    return [
        (place(s, 2 * p + i), place(s, 2 * p - 1 - i))
        for s in range(SECTIONS)
        for p in range(1, PAIRS)
        if p % 2 == parity
        for i in range(2)
    ]


def hop_sets(parity):
    return [
        (place(s, j), place(s - 1, j))
        for s in range(1, SECTIONS)
        if s % 2 == parity
        for j in range(SEGS)
    ]


def local(x, memory, weight, gain, probes, sharp, persistence, counts, slope):
    x, memory, weight, probes = x[0], memory[0, 0], weight[0], probes[0]
    decay = persistence[0, 0]
    section = lax.axis_index("section")
    seg = lax.axis_index("seg")
    pair = seg // 2

    n, qh, invq, rs, bdm, bdmh, bdph, invm, wr, ww, start = call(
        prepare_kernel,
        [
            ((ROWS, D), bf16), ((ROWS, D), bf16), ((ROWS, HEAD), f32), ((ROWS, HEAD), f32),
            ((GF, GF), bf16), ((GF, GF), bf16), ((GF, GF), bf16), ((MEM, HEAD), f32),
            ((ROWS, GF), bf16), ((ROWS, GF), bf16), ((ROWS, D), bf16),
        ],
        [VMEM, HBM] + [VMEM] * 4 + [SMEM] * 2,
        [pltpu.VMEM((GF, GF), bf16), pltpu.VMEM((D, D), bf16), pltpu.SemaphoreType.DMA],
        flops=2 * ROWS * D * D, moved=10 << 20,
    )(x, weight, gain, memory, probes, slope, sharp, counts)

    other = pair_swap(decay)
    one = jnp.ones_like(decay)
    none = jnp.zeros_like(decay)
    odd = seg % 2 == 1
    coefs = jnp.concatenate(
        [
            jnp.where(odd, other, one), jnp.where(odd, one, decay), jnp.where(odd, none, one),
            jnp.where(odd, one, other), decay * other, 1.0 - decay,
            jnp.broadcast_to(sharp * (1.0 / HEAD), decay.shape), none,
        ],
        axis=1,
    )

    def read(grad):
        return call(
            read_kernel,
            [((MEM, D), bf16), ((ROWS, GF), bf16)],
            [VMEM] * 7,
            flops=2 * ROWS * GF * D, moved=4 << 20,
        )(grad, wr, bdm, bdmh, qh, invm, coefs)

    def finish(mu, grad, ds):
        return call(
            finish_kernel,
            [((ROWS, D), bf16), ((MEM, D), bf16), ((MEM, D), bf16)],
            [HBM, VMEM, HBM, VMEM, HBM, HBM] + [VMEM] * 5 + [HBM] * 3,
            [
                pltpu.VMEM((D, D), bf16), pltpu.VMEM((GF, GF), bf16), pltpu.VMEM((ROWS, D), bf16),
                pltpu.VMEM((ROWS, D), f32), pltpu.VMEM((ROWS, D), bf16), pltpu.VMEM((ROWS, D), bf16),
                pltpu.VMEM((ROWS, D), bf16), pltpu.VMEM((MEM, D), f32), pltpu.VMEM((1, D), bf16),
                pltpu.VMEM((ROWS, HEAD), f32), pltpu.VMEM((ROWS, HEAD), f32),
                pltpu.SemaphoreType.DMA((7 + GROUPS,)),
            ],
            out=[HBM, ANY, ANY],
            flops=2 * ROWS * D * D, moved=12 << 20,
        )(mu, coefs, grad, n, x, gain, ww, ds, bdmh, bdph, qh, invq, rs, weight)

    def join(step, pair_sum, near, moving, mu, carry=None):
        got = [] if carry is None else [carry]
        count = 4 + len(got)
        return call(
            functools.partial(join_kernel, bool(got)),
            [((MEM, D), bf16), ((MEM, D), f32)],
            [SMEM] + [ANY] * (len(got) + 3) + [HBM] * 2,
            [pltpu.VMEM((MEM, D), bf16)] * 3
            + [
                pltpu.VMEM((MEM, HEAD), f32), pltpu.VMEM((MEM, D), bf16), pltpu.VMEM((MEM, D), f32),
                pltpu.SemaphoreType.DMA((8,)),
            ],
            moved=700 << 10, out=HBM, aliases={count: 0, count + 1: 1},
        )(step, pair_sum, near, coefs, *got, moving, mu)

    def blank(*kinds):
        return call(blank_kernel, kinds, [], out=HBM)()

    def first(grad):
        rho, ds = read(grad)
        near = pair_swap(rho)
        pair_sum = call(combine_kernel, [((MEM, D), bf16)], [VMEM] * 3, moved=400 << 10)(rho, near, coefs)[0]
        return pair_sum, near, ds

    def turn(grad):
        def body(step, held):
            moving, mu, ds, hidden = held
            step_now = jnp.reshape(step, (1,))

            def chain(sets):
                def run():
                    got = (lax.ppermute(moving, AXES, sets),) if sets else ()

                    def finishing():
                        new, *unused = finish(mu, grad, ds)
                        return (*unused, ds, new)

                    pair_sum, near, ds_, hidden_ = lax.cond(
                        step == 0, lambda: first(grad) + (hidden,), finishing
                    )
                    return (*join(step_now, pair_sum, near, moving, mu, *got), ds_, hidden_)
                return run

            sends = step == 1
            chain_to = jnp.where(
                pair == jnp.where(sends, 0, PAIRS - 1), 0, jnp.where((pair % 2 == 1) == sends, 1, 2)
            )
            return tuple(
                lax.switch(chain_to, [chain(None), chain(chain_sets(1)), chain(chain_sets(0))])
            )

        held = blank(((MEM, D), bf16), ((MEM, D), f32), ((ROWS, GF), bf16), ((ROWS, D), bf16))
        held = lax.fori_loop(0, two, body, tuple(held))
        return held[3], held[1]

    def hop(step, held):
        grad, hidden, mu = held
        sends = step == 1
        hop_to = jnp.where(
            section == jnp.where(sends, 0, SECTIONS - 1), 0, jnp.where((section % 2 == 1) == sends, 1, 2)
        )
        grad = lax.switch(
            hop_to,
            [
                lambda: grad,
                lambda: lax.ppermute(hidden, AXES, hop_sets(1)),
                lambda: lax.ppermute(hidden, AXES, hop_sets(0)),
            ],
        )
        hidden, mu = lax.cond(sends, lambda: (hidden, mu), lambda: tuple(turn(grad)))
        return grad, hidden, mu

    two = jnp.minimum(counts[0], 2)
    state = lax.fori_loop(
        0, two, hop, (start, *blank(((ROWS, D), bf16), ((MEM, D), f32)))
    )[1:]
    return state[0][None], state[1][None, None]


def solution(mesh):
    placed = (
        P("section", "seg", None),
        P("section", "seg", None, None),
        P("section", None, None),
        P("section", None),
        P("section", None, None),
        P("section", None),
        P("section", "seg", None, None),
        P("seg"),
        P("seg", None),
    )
    return jax.shard_map(
        local,
        mesh=mesh,
        in_specs=placed,
        out_specs=(P("section", "seg", None), P("section", "seg", None, None)),
        check_vma=False,
    )
```
